32 devices in a mesh: parts: 1, row: 4 (over z), col: 4 (over y, x), rep: 2 (over core).
Axes of the slice: x: 2, y: 2, z: 4, core: 2. Of those that a mesh axis runs over, the one named last changes fastest.
Arguments:
- feats: bfloat16 [4096, 128], P(('parts', 'row', 'col', 'rep')), may hold values from -6 to 6
- weight: bfloat16 [128, 256], replicated, may hold values from -0.5 to 0.5
- tile_vals: bfloat16 [2048, 128, 128], P(('parts', 'row', 'col', 'rep')), may hold values from -0.09375 to 0.09375
- tile_rows: int32 [2048], P(('parts', 'row', 'col', 'rep')), may hold values from 0 to 7
- tile_cols: int32 [2048], P(('parts', 'row', 'col', 'rep')), may hold values from 0 to 7
- tile_count: int32 [32], P(('parts', 'row', 'col', 'rep')), may hold values from 16 to 64, as said below
- relu_mask: int32 [4096, 256], P(('parts', 'row', 'col', 'rep')), may hold values 0 or 1
- cotangent: bfloat16 [4096, 256], P(('parts', 'row', 'col', 'rep')), may hold values from -6 to 6
Outputs:
- activated: bfloat16 [4096, 256], P(('parts', 'row', 'col', 'rep'))
- grad_w: float32 [128, 256], P('parts')
- grad_x: bfloat16 [4096, 128], P(('parts', 'row', 'col', 'rep'))
The draws below stay inside these ranges and needn't reach their ends.
Inputs may be any that keep to these rules, and one draw needn't show every extreme that they name: `tile_rows`: row block of a slot within its device's destination list. `tile_cols`: column block of a slot within its device's source list. `tile_count`: live slots are the first ones of a device; the rest are ignored; in every draw some device has all 64 slots live.
All inputs are finite; a program needn't handle non-finite values. No bound on the sum of `relu_mask` on one device may be relied on, other than what follows from the above.
Results may differ from the reference program's by a relative error of at most 0.005.
Values may be sent and summed in bfloat16 or wider, within the bound.
A program may use at most 64 MiB of HBM per device.

```python
import jax
import jax.numpy as jnp
from jax import lax

FEAT = 128
HID = 256
BLOCK = 128
NODE_DEV = 128
TILE_DEV = 64
GRID_DEVS = 32
NODES = 4096
TILES = 2048
ROW_BLOCKS = 8
COL_BLOCKS = 8
N_COL = 4
N_REP = 2


def draw_tile_count(key, part):
    key = jax.random.fold_in(key, 7)
    first, second, third = jax.random.split(key, 3)
    counts = jax.random.randint(first, (GRID_DEVS,), TILE_DEV // 4, TILE_DEV // 2 + 1)
    heavy = jax.random.randint(second, (GRID_DEVS,), 0, 8) == 0
    chosen = jax.random.randint(third, (), 0, GRID_DEVS)
    heavy = heavy | (jnp.arange(GRID_DEVS, dtype=jnp.int32) == chosen)
    return jnp.where(heavy, TILE_DEV, counts).astype(jnp.int32)


def place_ends(values, key, low, top_value):
    longest = values.shape.index(max(values.shape))
    spots = []
    for shift in (0, 1):
        where = [jax.random.randint(jax.random.fold_in(key, axis), (), 0, length) for axis, length in enumerate(values.shape)]
        where[longest] = (where[longest] + shift) % values.shape[longest]
        spots.append(tuple(where))
    return values.at[spots[0]].set(low).at[spots[1]].set(top_value)


def shard_levels(own_key, shape, pieces, least, top_value):
    def one(dim, blocks):
        draws = jax.random.uniform(jax.random.fold_in(jax.random.fold_in(own_key, 6), dim), (blocks,), jnp.float32, least / len(pieces), top_value / len(pieces))
        return jnp.repeat(jnp.exp(draws), shape[dim] // blocks).reshape((-1,) + (1,) * (len(shape) - dim - 1))

    gain = one(*pieces[0])
    for cut in pieces[1:]:
        gain = gain * one(*cut)
    return gain


def normal_values(key, shape, spread, reach, shards=(), held_as=jnp.bfloat16):
    drawn = jax.random.normal(key, shape, jnp.float32) * spread
    if len(shards) > 0:
        drawn = shard_levels(key, shape, shards, -0.22, 0.18) * drawn
    return jnp.clip(drawn, min=-reach, max=reach).astype(held_as)


def setup_inputs(seed: int = 0, part: int = 0) -> dict:
    streams_of = jax.random.split(jax.random.key(seed), 9)
    own_keys = jax.random.split(jax.random.fold_in(streams_of[8], part), 9)
    feats = normal_values(own_keys[0], (NODES, FEAT), 1.0, 6.0, ((0, 32),))
    weight = normal_values(streams_of[1], (FEAT, HID), FEAT ** -0.5, 0.5)
    tile_vals = normal_values(own_keys[2], (TILES, BLOCK, BLOCK), (TILE_DEV * BLOCK * BLOCK // (2 * NODE_DEV)) ** -0.5, 0.09375, ((0, 32),))
    tile_rows = place_ends(jax.random.randint(own_keys[3], (TILES,), 0, ROW_BLOCKS), jax.random.fold_in(own_keys[3], 1), 0, ROW_BLOCKS - 1).astype(jnp.int32)
    tile_cols = place_ends(jax.random.randint(own_keys[4], (TILES,), 0, COL_BLOCKS), jax.random.fold_in(own_keys[4], 1), 0, COL_BLOCKS - 1).astype(jnp.int32)
    tile_count = draw_tile_count(jax.random.fold_in(jax.random.fold_in(streams_of[8], part), 71), part)
    relu_mask = place_ends((jax.random.randint(own_keys[6], (NODES, HID), 0, 2) < 1).astype(jnp.int32), jax.random.fold_in(own_keys[6], 1), 0, 1)
    cotangent = normal_values(own_keys[7], (NODES, HID), 1.0, 6.0, ((0, 32),))
    return dict(feats=feats, weight=weight, tile_vals=tile_vals, tile_rows=tile_rows, tile_cols=tile_cols, tile_count=tile_count, relu_mask=relu_mask, cotangent=cotangent)


def reference(feats, weight, tile_vals, tile_rows, tile_cols, tile_count, relu_mask, cotangent):
    values = tile_vals.reshape(GRID_DEVS, TILE_DEV, BLOCK, BLOCK)
    row_ids = tile_rows.reshape(GRID_DEVS, TILE_DEV)
    col_ids = tile_cols.reshape(GRID_DEVS, TILE_DEV)
    lanes = jnp.arange(BLOCK, dtype=jnp.int32)
    devices = jnp.arange(GRID_DEVS, dtype=jnp.int32)

    def places(device, rows_here, cols_here):
        row_group = device // (N_COL * N_REP)
        col_group = (device // N_REP) % N_COL
        dest = row_group * (N_COL * N_REP * NODE_DEV) + rows_here[:, None] * BLOCK + lanes[None, :]
        position = cols_here[:, None] * BLOCK + lanes[None, :]
        piece = position // NODE_DEV
        owner = ((piece // N_REP) * N_COL + col_group) * N_REP + piece % N_REP
        source = owner * NODE_DEV + position % NODE_DEV
        live = (jnp.arange(TILE_DEV, dtype=jnp.int32) < tile_count[device]).astype(jnp.float32)
        return dest.astype(jnp.int32), source.astype(jnp.int32), live

    def forward_step(total, item):
        device, block_vals, rows_here, cols_here = item
        dest, source, live = places(device, rows_here, cols_here)
        inputs = feats[source].astype(jnp.float32)
        product = jnp.einsum("tij,tjf->tif", block_vals.astype(jnp.float32), inputs) * live[:, None, None]
        return total.at[dest.reshape(-1)].add(product.reshape(-1, FEAT)), None

    agg, _ = lax.scan(forward_step, jnp.zeros((NODES, FEAT), jnp.float32), (devices, values, row_ids, col_ids))
    agg_b = agg.astype(jnp.bfloat16)
    keep = relu_mask.astype(jnp.float32)
    hidden = jnp.dot(agg_b, weight, preferred_element_type=jnp.float32)
    activated = (hidden * keep).astype(jnp.bfloat16)
    grad_h = (cotangent.astype(jnp.float32) * keep).astype(jnp.bfloat16)
    grad_w = jnp.dot(agg_b.T, grad_h, preferred_element_type=jnp.float32) * (NODES ** -0.5)
    back = jnp.dot(grad_h, weight.T, preferred_element_type=jnp.float32).astype(jnp.bfloat16)

    def backward_step(total, item):
        device, block_vals, rows_here, cols_here = item
        dest, source, live = places(device, rows_here, cols_here)
        inputs = back[dest].astype(jnp.float32)
        product = jnp.einsum("tij,tif->tjf", block_vals.astype(jnp.float32), inputs) * live[:, None, None]
        return total.at[source.reshape(-1)].add(product.reshape(-1, FEAT)), None

    grad_acc, _ = lax.scan(backward_step, jnp.zeros((NODES, FEAT), jnp.float32), (devices, values, row_ids, col_ids))
    return activated, grad_w, grad_acc.astype(jnp.bfloat16)
```

```python
import functools

import jax
import jax.numpy as jnp
from jax import lax
from jax.experimental import pallas as pl
from jax.experimental.pallas import tpu as pltpu
from jax.sharding import PartitionSpec as P

FEAT = 128
BLOCK = 128
LANES = 128
SUBROWS = 16


def fused(
    rows_n, cols_n, reps_n, scale,
    feats, weight, tiles, tile_rows, tile_cols, count, mask, cot,
    act_o, gw_o, gx_o,
    wv, tv, mv, cv, rv, kv, idx_v, idx_s, chain, a_send, a_recv, a_mat,
    f_buf, b_buf, agg_s, agg_r, gx_s, gx_r, gw_s, gw_r, gw_b,
    loc, idx_sem, fs, fr, bs, br, as_, ar, gs, gr, xs, xr, ws1, wr1, ws2, wr2,
):
    part = lax.axis_index("parts")
    r = lax.axis_index("row")
    c = lax.axis_index("col")
    p = lax.axis_index("rep")
    plane = cols_n * reps_n
    total = rows_n * plane
    chips = rows_n * cols_n
    q = c * reps_n + p
    me = r * plane + q
    chip = r * cols_n + c
    slots = tiles.shape[0]
    row_blocks = plane
    col_blocks = rows_n * reps_n

    def at(flat):
        return (part, flat // plane, (flat // reps_n) % cols_n, flat % reps_n)

    def remote(src, dst, send, recv, device):
        return pltpu.make_async_remote_copy(
            src_ref=src, dst_ref=dst, send_sem=send, recv_sem=recv,
            device_id=device, device_id_type=pl.DeviceIdType.MESH,
        )

    barrier = pltpu.get_barrier_semaphore()

    @pl.loop(1, total)
    def _(k):
        pl.semaphore_signal(
            barrier, inc=1, device_id=at(lax.rem(me + k, total)),
            device_id_type=pl.DeviceIdType.MESH,
        )

    own_feats = f_buf.at[pl.ds(pl.multiple_of(r * BLOCK, BLOCK), BLOCK)]
    loads = [
        pltpu.make_async_copy(src, dst, loc.at[i])
        for i, (src, dst) in enumerate(
            [(tile_rows, rv), (tile_cols, kv), (mask, mv), (cot, cv), (weight, wv),
             (feats, own_feats), (tiles, tv)]
        )
    ]
    for copy in loads:
        copy.start()

    loads[0].wait()
    loads[1].wait()
    key = rv[...] * col_blocks + kv[...]
    shape = (slots, LANES)
    lane = lax.broadcasted_iota(jnp.int32, shape, 1)
    sub = lax.broadcasted_iota(jnp.int32, shape, 0)
    wide = jnp.concatenate([key, jnp.full((1, LANES - slots), -1, jnp.int32)], axis=1)
    wide = jnp.broadcast_to(wide, shape)
    tall = jnp.sum(jnp.where(lane == sub, wide, 0), axis=1, keepdims=True)
    prev = jnp.where((tall == wide) & (sub < lane), sub + 1, 0)
    last = jnp.where((tall == lane) & (sub < count[0]), sub + 1, 0)
    idx_v[...] = jnp.zeros_like(idx_v)
    idx_v[0:1, :] = jnp.max(prev, axis=0, keepdims=True)
    idx_v[1:2, :] = jnp.max(last, axis=0, keepdims=True)
    idx_copy = pltpu.make_async_copy(idx_v, idx_s, idx_sem)
    idx_copy.start()

    for copy in loads[2:6]:
        copy.wait()
    keep = mv[...].astype(jnp.float32)
    grad_h = (cv[...].astype(jnp.float32) * keep).astype(jnp.bfloat16)
    b_buf[q] = lax.dot_general(
        wv[...], grad_h, (((1,), (1,)), ((), ())), preferred_element_type=jnp.float32
    ).astype(jnp.bfloat16)

    pl.semaphore_wait(barrier, total - 1)

    f_copies = []
    for k in range(1, rows_n):
        copy = remote(
            own_feats, own_feats, fs.at[k], fr.at[k],
            (part, lax.rem(r + k, rows_n), c, p),
        )
        copy.start()
        f_copies.append(copy)
    b_copies = []
    for k in range(1, plane):
        other = lax.rem(q + k, plane)
        copy = remote(
            b_buf.at[q], b_buf.at[q], bs.at[k], br.at[k],
            (part, r, other // reps_n, other % reps_n),
        )
        copy.start()
        b_copies.append(copy)

    loads[6].wait()
    idx_copy.wait()
    chain[0] = jnp.zeros((BLOCK, BLOCK), jnp.float32)

    @pl.loop(0, slots)
    def _(t):
        chain[t + 1] = chain[idx_s[0, t]] + tv[t].astype(jnp.float32)

    chunk = reps_n * BLOCK
    a_copies = []
    for k in range(cols_n):
        dest = lax.rem(c + 1 + k, cols_n)
        for j in range(reps_n):
            for i in range(rows_n):
                cell = (dest * reps_n + j) * col_blocks + i * reps_n + (1 - p)
                a_send[k, pl.ds(j * BLOCK, BLOCK), pl.ds(i * BLOCK, BLOCK)] = chain[
                    idx_s[1, cell]
                ].astype(jnp.bfloat16)
        copy = remote(a_send.at[k], a_recv.at[k], as_.at[k], ar.at[k], (part, r, c, 1 - p))
        copy.start()
        a_copies.append(copy)

    for copy in f_copies:
        copy.wait_recv()
    g_copies = []
    for k in range(cols_n):
        dest = lax.rem(c + 1 + k, cols_n)
        a_copies[k].wait_recv()
        for j in range(reps_n):
            for i in range(rows_n):
                cell = (dest * reps_n + j) * col_blocks + i * reps_n + p
                spot = (pl.ds(j * BLOCK, BLOCK), pl.ds(i * BLOCK, BLOCK))
                a_mat[(k, *spot)] = (
                    chain[idx_s[1, cell]] + a_recv[(k, *spot)].astype(jnp.float32)
                ).astype(jnp.bfloat16)
        partial = jnp.dot(
            a_mat[k], f_buf[...], preferred_element_type=jnp.float32
        ).astype(jnp.bfloat16)
        for j in range(reps_n):
            agg_s[k * reps_n + j] = partial[j * BLOCK:(j + 1) * BLOCK]
        targets = range(reps_n) if k < cols_n - 1 else [1 - p]
        for j in targets:
            copy = remote(
                agg_s.at[k * reps_n + j], agg_r.at[q], gs.at[k * reps_n + j], gr.at[q],
                (part, r, dest, j),
            )
            copy.start()
            g_copies.append(copy)

    for copy in b_copies:
        copy.wait_recv()
    grad_t = jnp.zeros((FEAT, rows_n * BLOCK), jnp.float32)
    for k in range(cols_n):
        dest = lax.rem(c + 1 + k, cols_n)
        pair = jnp.concatenate([b_buf[dest * reps_n + j] for j in range(reps_n)], axis=1)
        grad_t += jnp.dot(pair, a_mat[k], preferred_element_type=jnp.float32)
    for i in range(rows_n):
        gx_s[i] = grad_t[:, i * BLOCK:(i + 1) * BLOCK].astype(jnp.bfloat16)
    x_copies = []
    for k in range(1, rows_n):
        other = lax.rem(r + k, rows_n)
        copy = remote(gx_s.at[other], gx_r.at[k], xs.at[k], xr.at[k], (part, other, c, p))
        copy.start()
        x_copies.append(copy)

    agg = agg_s[(cols_n - 1) * reps_n + p].astype(jnp.float32)
    for k in range(1, plane):
        other = lax.rem(q + k, plane)
        remote(agg_s.at[0], agg_r.at[other], gs.at[0], gr.at[other], (part, r, c, 1 - p)).wait_recv()
        agg += agg_r[other].astype(jnp.float32)
    agg_b = agg.astype(jnp.bfloat16)
    term = lax.dot_general(
        agg_b, grad_h, (((0,), (0,)), ((), ())), preferred_element_type=jnp.float32
    ).astype(jnp.bfloat16)
    per_half = FEAT // SUBROWS
    for s in range(chips):
        lo, half = (s % per_half) * SUBROWS, (s // per_half) * LANES
        gw_s[s] = term[lo:lo + SUBROWS, half:half + LANES]

    @pl.loop(1, chips)
    def _(k):
        other = lax.rem(chip + k, chips)
        remote(
            gw_s.at[other], gw_r.at[me], ws1, wr1, (part, other // cols_n, other % cols_n, 0)
        ).start()

    @pl.when(p != 0)
    def _():
        remote(gw_s.at[chip], gw_r.at[me], ws1, wr1, (part, r, c, 0)).start()

    hidden = jnp.dot(agg_b, wv[...], preferred_element_type=jnp.float32)
    act_o[...] = (hidden * keep).astype(jnp.bfloat16)

    grad_t = gx_s[r].astype(jnp.float32)
    for k, copy in enumerate(x_copies):
        copy.wait_recv()
        grad_t += gx_r[k + 1].astype(jnp.float32)
    gx_o[...] = grad_t.T.astype(jnp.bfloat16)

    @pl.when(p == 0)
    def _():
        gw_r[me] = gw_s[chip]
        rest = gw_r.at[pl.ds(0, total - 1)]
        remote(rest, rest, ws1, wr1, (part, r, c, 1 - p)).wait_recv()
        terms = jnp.sum(gw_r[...].astype(jnp.float32), axis=0)
        gw_b[chip] = (terms * scale).astype(jnp.bfloat16)

        @pl.loop(1, total)
        def _(k):
            remote(gw_b.at[chip], gw_b.at[chip], ws2, wr2, at(lax.rem(me + k, total))).start()

        rest = gw_b.at[pl.ds(0, chips - 1)]
        remote(rest, rest, ws2, wr2, (part, r, c, 1 - p)).wait_recv()
        sent = gw_r.at[pl.ds(0, total - 1)]
        remote(sent, sent, ws2, wr2, (part, r, c, 1 - p)).wait_send()
        sent = gw_s.at[pl.ds(0, chips - 1)]
        remote(sent, sent, ws1, wr1, (part, r, c, 1 - p)).wait_send()

    @pl.when(p != 0)
    def _():
        remote(gw_b, gw_b, ws2, wr2, (part, r, c, 0)).wait_recv()
        remote(gw_s, gw_s, ws1, wr1, (part, r, c, 0)).wait_send()

    for s in range(chips):
        lo, half = (s % per_half) * SUBROWS, (s // per_half) * LANES
        gw_o[lo:lo + SUBROWS, half:half + LANES] = gw_b[s].astype(jnp.float32)

    for copy in f_copies + b_copies + a_copies + g_copies + x_copies:
        copy.wait_send()


def fused_body(rows_n, cols_n, reps_n, *args):
    feats, weight, tiles, tile_rows, tile_cols, count, mask, cot = args
    slots = tiles.shape[0]
    hid = weight.shape[1]
    plane = cols_n * reps_n
    total = rows_n * plane
    chips = rows_n * cols_n
    nodes = feats.shape[0] * total
    half = rows_n * BLOCK
    b16, f32, i32 = jnp.bfloat16, jnp.float32, jnp.int32
    dma = pltpu.SemaphoreType.DMA
    anywhere = pl.BlockSpec(memory_space=pl.ANY)
    vmem = pl.BlockSpec(memory_space=pltpu.VMEM)
    return tuple(pl.pallas_call(
        functools.partial(fused, rows_n, cols_n, reps_n, float(nodes) ** -0.5),
        out_shape=(
            jax.ShapeDtypeStruct((BLOCK, hid), b16),
            jax.ShapeDtypeStruct((FEAT, hid), f32),
            jax.ShapeDtypeStruct((BLOCK, FEAT), b16),
        ),
        in_specs=[anywhere] * 5 + [pl.BlockSpec(memory_space=pltpu.SMEM)] + [anywhere] * 2,
        out_specs=(vmem, vmem, vmem),
        scratch_shapes=[
            pltpu.VMEM((FEAT, hid), b16),
            pltpu.VMEM((slots, BLOCK, BLOCK), b16),
            pltpu.VMEM((BLOCK, hid), i32),
            pltpu.VMEM((BLOCK, hid), b16),
            pltpu.VMEM((1, slots), i32),
            pltpu.VMEM((1, slots), i32),
            pltpu.VMEM((8, LANES), i32),
            pltpu.SMEM((8, LANES), i32),
            pltpu.VMEM((slots + 1, BLOCK, BLOCK), f32),
            pltpu.VMEM((cols_n, reps_n * BLOCK, half), b16),
            pltpu.VMEM((cols_n, reps_n * BLOCK, half), b16),
            pltpu.VMEM((cols_n, reps_n * BLOCK, half), b16),
            pltpu.VMEM((half, FEAT), b16),
            pltpu.VMEM((plane, FEAT, BLOCK), b16),
            pltpu.VMEM((plane, BLOCK, FEAT), b16),
            pltpu.VMEM((plane, BLOCK, FEAT), b16),
            pltpu.VMEM((rows_n, FEAT, BLOCK), b16),
            pltpu.VMEM((rows_n, FEAT, BLOCK), b16),
            pltpu.VMEM((chips, SUBROWS, LANES), b16),
            pltpu.VMEM((total, SUBROWS, LANES), b16),
            pltpu.VMEM((chips, SUBROWS, LANES), b16),
            dma((7,)), dma,
            dma((rows_n,)), dma((rows_n,)),
            dma((plane,)), dma((plane,)),
            dma((cols_n,)), dma((cols_n,)),
            dma((plane,)), dma((plane,)),
            dma((rows_n,)), dma((rows_n,)),
            dma, dma, dma, dma,
        ],
        compiler_params=pltpu.CompilerParams(
            collective_id=0, has_side_effects=True, vmem_limit_bytes=40 * 1024 * 1024
        ),
    )(
        feats, weight, tiles, tile_rows.reshape(1, slots), tile_cols.reshape(1, slots),
        count, mask, cot,
    ))


def fits(mesh, args):
    rows_n, cols_n, reps_n = (mesh.shape[name] for name in ("row", "col", "rep"))
    total = rows_n * cols_n * reps_n
    hid = args[1].shape[1]
    per_chip = SUBROWS * LANES * rows_n * cols_n
    cells = rows_n * reps_n * cols_n * reps_n
    return (
        reps_n == 2
        and cells <= LANES
        and args[2].shape[0] // (total * mesh.shape["parts"]) <= LANES // 2
        and args[0].shape[0] == total * BLOCK * mesh.shape["parts"]
        and FEAT * hid == per_chip
    )


tiles_per_turn = 4


def run_tiles(locate, finish, step_fn, init):
    turns = (finish + tiles_per_turn - 1) // tiles_per_turn

    def turn(index, carry):
        slots = index * tiles_per_turn + jnp.arange(tiles_per_turn, dtype=jnp.int32)
        live = slots < finish
        values, rows_here, cols_here = locate(slots)
        return step_fn(carry, values, rows_here, cols_here, live)

    return lax.fori_loop(0, turns, turn, init)


def body(feats, weight, tile_vals, tile_rows, tile_cols, tile_count, relu_mask, cotangent):
    slot_total = tile_vals.shape[0]
    rep_count = lax.axis_size("rep")
    row_count = lax.axis_size("row")
    node_dev = feats.shape[0]
    row_blocks = node_dev * lax.axis_size("col") * rep_count // BLOCK
    own_count = tile_count[0]

    def locate(slots):
        place = jnp.minimum(slots, slot_total - 1)
        return (
            jnp.take(tile_vals, place, axis=0),
            jnp.take(tile_rows, place),
            jnp.take(tile_cols, place),
        )

    gathered = lax.all_gather(feats, ("row", "rep"), axis=0, tiled=True)
    source_blocks = gathered.reshape(-1, BLOCK, FEAT)
    col_blocks = source_blocks.shape[0]

    def forward_step(total, values, rows_here, cols_here, live):
        inputs = jnp.take(source_blocks, cols_here, axis=0)
        product = jnp.einsum("tij,tjf->tif", values, inputs, preferred_element_type=jnp.float32)
        product = product * live.astype(jnp.float32)[:, None, None]
        return total.at[rows_here].add(product)

    dest_part = run_tiles(
        locate, own_count, forward_step, jnp.zeros((row_blocks, BLOCK, FEAT), jnp.float32)
    )
    agg = lax.psum_scatter(
        dest_part.reshape(row_blocks * BLOCK, FEAT), ("col", "rep"), scatter_dimension=0, tiled=True
    )
    agg_b = agg.astype(jnp.bfloat16)
    keep = relu_mask.astype(jnp.float32)
    hidden = jnp.dot(agg_b, weight, preferred_element_type=jnp.float32)
    activated = (hidden * keep).astype(jnp.bfloat16)
    grad_h = (cotangent.astype(jnp.float32) * keep).astype(jnp.bfloat16)
    weight_term = lax.dot_general(
        agg_b, grad_h, (((0,), (0,)), ((), ())), preferred_element_type=jnp.float32
    )
    node_total = node_dev * row_count * lax.axis_size("col") * rep_count
    grad_w = lax.psum(weight_term, ("row", "col", "rep")) * float(node_total) ** (-0.5)
    back = lax.dot_general(
        grad_h, weight, (((1,), (1,)), ((), ())), preferred_element_type=jnp.float32
    ).astype(jnp.bfloat16)
    dest_blocks = lax.all_gather(back, ("col", "rep"), axis=0, tiled=True).reshape(
        row_blocks, BLOCK, FEAT
    )

    def backward_step(total, values, rows_here, cols_here, live):
        inputs = jnp.take(dest_blocks, rows_here, axis=0)
        product = jnp.einsum("tij,tif->tjf", values, inputs, preferred_element_type=jnp.float32)
        product = product * live.astype(jnp.float32)[:, None, None]
        return total.at[cols_here].add(product)

    source_part = run_tiles(
        locate, own_count, backward_step, jnp.zeros((col_blocks, BLOCK, FEAT), jnp.float32)
    )
    grad_acc = lax.psum_scatter(
        source_part.reshape(col_blocks * BLOCK, FEAT),
        ("row", "rep"),
        scatter_dimension=0,
        tiled=True,
    )
    return (activated, grad_w, grad_acc.astype(jnp.bfloat16))


def solution(mesh):
    sizes = tuple(mesh.shape[name] for name in ("row", "col", "rep"))
    spread = ("parts", "row", "col", "rep")
    placed = (
        P(spread, None), P(), P(spread, None, None), P(spread), P(spread), P(spread),
        P(spread, None), P(spread, None),
    )

    def whole(*args):
        local = functools.partial(fused_body, *sizes) if fits(mesh, args) else body
        return jax.shard_map(
            local,
            mesh=mesh,
            in_specs=placed,
            out_specs=(P(spread, None), P("parts", None), P(spread, None)),
            check_vma=False,
        )(*args)

    return whole
```

```python
import functools

import jax
import jax.numpy as jnp
from jax import lax
from jax.experimental import pallas as pl
from jax.experimental.pallas import tpu as pltpu
from jax.sharding import PartitionSpec as P

FEAT = 128
BLOCK = 128
LANES = 128
SUBROWS = 16
VMEM_LIMIT = 60 * 1024 * 1024


def fused(
    rows_n, cols_n, reps_n, scale,
    feats, weight, tiles, tile_rows, tile_cols, count, mask, cot,
    act_o, gw_o, gx_o,
    wv, tv, mv, cv, rv, kv, idx_v, idx_s, chain, a_send, a_recv, a_mat,
    f_buf, b_buf, agg_s, agg_r, gx_s, gx_r, gw_s, gw_r, gw_z, gw_b, act_v, gx_v,
    loc, idx_sem, fs, fr, bs, br, as_, ar, gs, gr, xs, xr, ws1, wr1, ws2, wr2, ws3, wr3,
):
    part = lax.axis_index("parts")
    r = lax.axis_index("row")
    c = lax.axis_index("col")
    p = lax.axis_index("rep")
    plane = cols_n * reps_n
    q = c * reps_n + p
    slots = tiles.shape[0]
    row_blocks = plane
    col_blocks = rows_n * reps_n

    def remote(src, dst, send, recv, device):
        return pltpu.make_async_remote_copy(
            src_ref=src, dst_ref=dst, send_sem=send, recv_sem=recv,
            device_id=device, device_id_type=pl.DeviceIdType.MESH,
        )

    barrier = pltpu.get_barrier_semaphore()

    def plane_peer(k):
        other = lax.rem(q + k, plane)
        return other, (part, r, other // reps_n, other % reps_n)

    def row_peer(k):
        other = lax.rem(r + k, rows_n)
        return other, (part, other, c, p)

    for k in range(1, plane):
        pl.semaphore_signal(
            barrier, inc=1, device_id=plane_peer(k)[1], device_id_type=pl.DeviceIdType.MESH
        )
    for k in range(1, rows_n):
        pl.semaphore_signal(
            barrier, inc=1, device_id=row_peer(k)[1], device_id_type=pl.DeviceIdType.MESH
        )

    own_feats = f_buf.at[pl.ds(pl.multiple_of(r * BLOCK, BLOCK), BLOCK)]
    loads = [
        pltpu.make_async_copy(src, dst, loc.at[i])
        for i, (src, dst) in enumerate(
            [(tile_rows, rv), (tile_cols, kv), (mask, mv), (cot, cv), (weight, wv),
             (feats, own_feats), (tiles, tv)]
        )
    ]
    for copy in loads:
        copy.start()

    loads[0].wait()
    loads[1].wait()
    key = rv[...] * col_blocks + kv[...]
    shape = (slots, LANES)
    lane = lax.broadcasted_iota(jnp.int32, shape, 1)
    sub = lax.broadcasted_iota(jnp.int32, shape, 0)
    wide = jnp.concatenate([key, jnp.full((1, LANES - slots), -1, jnp.int32)], axis=1)
    wide = jnp.broadcast_to(wide, shape)
    tall = jnp.sum(jnp.where(lane == sub, wide, 0), axis=1, keepdims=True)
    prev = jnp.where((tall == wide) & (sub < lane), sub + 1, 0)
    last = jnp.where((tall == lane) & (sub < count[0]), sub + 1, 0)
    idx_v[...] = jnp.zeros_like(idx_v)
    idx_v[0:1, :] = jnp.max(prev, axis=0, keepdims=True)
    idx_v[1:2, :] = jnp.max(last, axis=0, keepdims=True)
    idx_copy = pltpu.make_async_copy(idx_v, idx_s, idx_sem)
    idx_copy.start()

    for copy in loads[2:6]:
        copy.wait()
    keep = mv[...].astype(jnp.float32)
    grad_h = (cv[...].astype(jnp.float32) * keep).astype(jnp.bfloat16)
    b_buf[q] = lax.dot_general(
        wv[...], grad_h, (((1,), (1,)), ((), ())), preferred_element_type=jnp.float32
    ).astype(jnp.bfloat16)

    pl.semaphore_wait(barrier, plane + rows_n - 2)

    f_copies = []
    for k in range(1, rows_n):
        copy = remote(
            own_feats, own_feats, fs.at[k], fr.at[k],
            (part, lax.rem(r + k, rows_n), c, p),
        )
        copy.start()
        f_copies.append(copy)
    b_copies = []
    for k in range(1, plane):
        other = lax.rem(q + k, plane)
        copy = remote(
            b_buf.at[q], b_buf.at[q], bs.at[k], br.at[k],
            (part, r, other // reps_n, other % reps_n),
        )
        copy.start()
        b_copies.append(copy)

    loads[6].wait()
    idx_copy.wait()
    chain[0] = jnp.zeros((BLOCK, BLOCK), jnp.float32)

    @pl.loop(0, slots)
    def _(t):
        chain[t + 1] = chain[idx_s[0, t]] + tv[t].astype(jnp.float32)

    chunk = reps_n * BLOCK
    a_copies = []
    for k in range(cols_n):
        dest = lax.rem(c + 1 + k, cols_n)
        for j in range(reps_n):
            for i in range(rows_n):
                cell = (dest * reps_n + j) * col_blocks + i * reps_n + (1 - p)
                a_send[k, pl.ds(j * BLOCK, BLOCK), pl.ds(i * BLOCK, BLOCK)] = chain[
                    idx_s[1, cell]
                ].astype(jnp.bfloat16)
        copy = remote(a_send.at[k], a_recv.at[k], as_.at[k], ar.at[k], (part, r, c, 1 - p))
        copy.start()
        a_copies.append(copy)

    for copy in f_copies:
        copy.wait_recv()
    g_copies = []
    for k in range(cols_n):
        dest = lax.rem(c + 1 + k, cols_n)
        a_copies[k].wait_recv()
        for j in range(reps_n):
            for i in range(rows_n):
                cell = (dest * reps_n + j) * col_blocks + i * reps_n + p
                spot = (pl.ds(j * BLOCK, BLOCK), pl.ds(i * BLOCK, BLOCK))
                a_mat[(k, *spot)] = (
                    chain[idx_s[1, cell]] + a_recv[(k, *spot)].astype(jnp.float32)
                ).astype(jnp.bfloat16)
        partial = jnp.dot(
            a_mat[k], f_buf[...], preferred_element_type=jnp.float32
        ).astype(jnp.bfloat16)
        for j in range(reps_n):
            agg_s[k * reps_n + j] = partial[j * BLOCK:(j + 1) * BLOCK]
        targets = range(reps_n) if k < cols_n - 1 else [1 - p]
        for j in targets:
            copy = remote(
                agg_s.at[k * reps_n + j], agg_r.at[q], gs.at[k * reps_n + j], gr.at[q],
                (part, r, dest, j),
            )
            copy.start()
            g_copies.append(copy)

    for copy in b_copies:
        copy.wait_recv()
    grad_t = jnp.zeros((FEAT, rows_n * BLOCK), jnp.float32)
    for k in range(cols_n):
        dest = lax.rem(c + 1 + k, cols_n)
        pair = jnp.concatenate([b_buf[dest * reps_n + j] for j in range(reps_n)], axis=1)
        grad_t += jnp.dot(pair, a_mat[k], preferred_element_type=jnp.float32)
    for i in range(rows_n):
        gx_s[i] = grad_t[:, i * BLOCK:(i + 1) * BLOCK].astype(jnp.bfloat16)
    x_copies = []
    for k in range(1, rows_n):
        other = lax.rem(r + k, rows_n)
        copy = remote(gx_s.at[other], gx_r.at[k], xs.at[k], xr.at[k], (part, other, c, p))
        copy.start()
        x_copies.append(copy)

    agg = agg_s[(cols_n - 1) * reps_n + p].astype(jnp.float32)
    for k in range(1, plane):
        other = lax.rem(q + k, plane)
        remote(agg_s.at[0], agg_r.at[other], gs.at[0], gr.at[other], (part, r, c, 1 - p)).wait_recv()
        agg += agg_r[other].astype(jnp.float32)
    agg_b = agg.astype(jnp.bfloat16)
    term = lax.dot_general(
        agg_b, grad_h, (((0,), (0,)), ((), ())), preferred_element_type=jnp.float32
    ).astype(jnp.bfloat16)
    piece = FEAT // plane
    for i in range(plane):
        gw_s[i] = term[i * piece:(i + 1) * piece]
    w_copies = []
    for k in range(1, plane):
        other, device = plane_peer(k)
        copy = remote(gw_s.at[other], gw_r.at[k], ws1.at[k], wr1.at[k], device)
        copy.start()
        w_copies.append(copy)

    hidden = jnp.dot(agg_b, wv[...], preferred_element_type=jnp.float32)
    act_v[...] = (hidden * keep).astype(jnp.bfloat16)
    stores = [
        pltpu.make_async_copy(act_v, act_o, loc.at[0]),
        pltpu.make_async_copy(gx_v, gx_o, loc.at[1]),
    ]
    stores[0].start()

    slab = gw_s[q].astype(jnp.float32)
    for k in range(1, plane):
        w_copies[k - 1].wait_recv()
        slab += gw_r[k].astype(jnp.float32)
    gw_z[r] = slab
    z_copies = []
    for k in range(1, rows_n):
        copy = remote(gw_z.at[r], gw_z.at[r], ws2.at[k], wr2.at[k], row_peer(k)[1])
        copy.start()
        z_copies.append(copy)
    for copy in z_copies:
        copy.wait_recv()
    gw_b[q] = (jnp.sum(gw_z[...], axis=0) * scale).astype(jnp.bfloat16)
    o_copies = []
    for k in range(1, plane):
        copy = remote(gw_b.at[q], gw_b.at[q], ws3.at[k], wr3.at[k], plane_peer(k)[1])
        copy.start()
        o_copies.append(copy)

    grad_t = gx_s[r].astype(jnp.float32)
    for k, copy in enumerate(x_copies):
        copy.wait_recv()
        grad_t += gx_r[k + 1].astype(jnp.float32)
    gx_v[...] = grad_t.T.astype(jnp.bfloat16)
    stores[1].start()

    for copy in o_copies:
        copy.wait_recv()
    stores.append(pltpu.make_async_copy(gw_b, gw_o, loc.at[2]))
    stores[2].start()

    for copy in w_copies + z_copies + o_copies:
        copy.wait_send()
    for copy in stores:
        copy.wait()
    for copy in f_copies + b_copies + a_copies + g_copies + x_copies:
        copy.wait_send()


def hand_over(act, gw, gx, act_o, gw_o, gx_o, act_v, gw_v, gx_v, wide_v, sems):
    loads = [
        pltpu.make_async_copy(src, dst, sems.at[i])
        for i, (src, dst) in enumerate([(gw, gw_v), (act, act_v), (gx, gx_v)])
    ]
    stores = [
        pltpu.make_async_copy(src, dst, sems.at[3 + i])
        for i, (src, dst) in enumerate([(wide_v, gw_o), (act_v, act_o), (gx_v, gx_o)])
    ]
    for copy in loads:
        copy.start()
    loads[0].wait()
    piece = gw_v.shape[1]
    for i in range(gw_v.shape[0]):
        wide_v[i * piece:(i + 1) * piece, :] = gw_v[i].astype(jnp.float32)
    stores[0].start()
    for load, store in zip(loads[1:], stores[1:]):
        load.wait()
        store.start()
    for copy in stores:
        copy.wait()


def fused_body(rows_n, cols_n, reps_n, *args):
    feats, weight, tiles, tile_rows, tile_cols, count, mask, cot = args
    slots = tiles.shape[0]
    hid = weight.shape[1]
    plane = cols_n * reps_n
    total = rows_n * plane
    nodes = feats.shape[0] * total
    half = rows_n * BLOCK
    b16, f32, i32 = jnp.bfloat16, jnp.float32, jnp.int32
    dma = pltpu.SemaphoreType.DMA
    anywhere = pl.BlockSpec(memory_space=pl.ANY)
    results = pl.pallas_call(
        functools.partial(fused, rows_n, cols_n, reps_n, float(nodes) ** -0.5),
        out_shape=(
            jax.ShapeDtypeStruct((BLOCK, hid), b16),
            jax.ShapeDtypeStruct((plane, FEAT // plane, hid), b16),
            jax.ShapeDtypeStruct((BLOCK, FEAT), b16),
        ),
        in_specs=[anywhere] * 5 + [pl.BlockSpec(memory_space=pltpu.SMEM)] + [anywhere] * 2,
        out_specs=(anywhere,) * 3,
        scratch_shapes=[
            pltpu.VMEM((FEAT, hid), b16),
            pltpu.VMEM((slots, BLOCK, BLOCK), b16),
            pltpu.VMEM((BLOCK, hid), i32),
            pltpu.VMEM((BLOCK, hid), b16),
            pltpu.VMEM((1, slots), i32),
            pltpu.VMEM((1, slots), i32),
            pltpu.VMEM((8, LANES), i32),
            pltpu.SMEM((8, LANES), i32),
            pltpu.VMEM((slots + 1, BLOCK, BLOCK), f32),
            pltpu.VMEM((cols_n, reps_n * BLOCK, half), b16),
            pltpu.VMEM((cols_n, reps_n * BLOCK, half), b16),
            pltpu.VMEM((cols_n, reps_n * BLOCK, half), b16),
            pltpu.VMEM((half, FEAT), b16),
            pltpu.VMEM((plane, FEAT, BLOCK), b16),
            pltpu.VMEM((plane, BLOCK, FEAT), b16),
            pltpu.VMEM((plane, BLOCK, FEAT), b16),
            pltpu.VMEM((rows_n, FEAT, BLOCK), b16),
            pltpu.VMEM((rows_n, FEAT, BLOCK), b16),
            pltpu.VMEM((plane, FEAT // plane, hid), b16),
            pltpu.VMEM((plane, FEAT // plane, hid), b16),
            pltpu.VMEM((rows_n, FEAT // plane, hid), f32),
            pltpu.VMEM((plane, FEAT // plane, hid), b16),
            pltpu.VMEM((BLOCK, hid), b16),
            pltpu.VMEM((BLOCK, FEAT), b16),
            dma((7,)), dma,
            dma((rows_n,)), dma((rows_n,)),
            dma((plane,)), dma((plane,)),
            dma((cols_n,)), dma((cols_n,)),
            dma((plane,)), dma((plane,)),
            dma((rows_n,)), dma((rows_n,)),
            dma((plane,)), dma((plane,)),
            dma((rows_n,)), dma((rows_n,)),
            dma((plane,)), dma((plane,)),
        ],
        compiler_params=pltpu.CompilerParams(
            collective_id=0, has_side_effects=True, vmem_limit_bytes=VMEM_LIMIT
        ),
    )(
        feats, weight, tiles, tile_rows.reshape(1, slots), tile_cols.reshape(1, slots),
        count, mask, cot,
    )
    return tuple(pl.pallas_call(
        hand_over,
        out_shape=(
            jax.ShapeDtypeStruct((BLOCK, hid), b16),
            jax.ShapeDtypeStruct((FEAT, hid), f32),
            jax.ShapeDtypeStruct((BLOCK, FEAT), b16),
        ),
        in_specs=[anywhere] * 3,
        out_specs=(anywhere,) * 3,
        scratch_shapes=[
            pltpu.VMEM((BLOCK, hid), b16),
            pltpu.VMEM((plane, FEAT // plane, hid), b16),
            pltpu.VMEM((BLOCK, FEAT), b16),
            pltpu.VMEM((FEAT, hid), f32),
            dma((6,)),
        ],
        compiler_params=pltpu.CompilerParams(vmem_limit_bytes=VMEM_LIMIT),
    )(*results))


def fits(mesh, args):
    rows_n, cols_n, reps_n = (mesh.shape[name] for name in ("row", "col", "rep"))
    total = rows_n * cols_n * reps_n
    cells = rows_n * reps_n * cols_n * reps_n
    return (
        reps_n == 2
        and cells <= LANES
        and args[2].shape[0] // (total * mesh.shape["parts"]) <= LANES // 2
        and args[0].shape[0] == total * BLOCK * mesh.shape["parts"]
        and FEAT % (SUBROWS * cols_n * reps_n) == 0
    )


tiles_per_turn = 4


def run_tiles(locate, finish, step_fn, init):
    turns = (finish + tiles_per_turn - 1) // tiles_per_turn

    def turn(index, carry):
        slots = index * tiles_per_turn + jnp.arange(tiles_per_turn, dtype=jnp.int32)
        live = slots < finish
        values, rows_here, cols_here = locate(slots)
        return step_fn(carry, values, rows_here, cols_here, live)

    return lax.fori_loop(0, turns, turn, init)


def body(feats, weight, tile_vals, tile_rows, tile_cols, tile_count, relu_mask, cotangent):
    slot_total = tile_vals.shape[0]
    rep_count = lax.axis_size("rep")
    row_count = lax.axis_size("row")
    node_dev = feats.shape[0]
    row_blocks = node_dev * lax.axis_size("col") * rep_count // BLOCK
    own_count = tile_count[0]

    def locate(slots):
        place = jnp.minimum(slots, slot_total - 1)
        return (
            jnp.take(tile_vals, place, axis=0),
            jnp.take(tile_rows, place),
            jnp.take(tile_cols, place),
        )

    gathered = lax.all_gather(feats, ("row", "rep"), axis=0, tiled=True)
    source_blocks = gathered.reshape(-1, BLOCK, FEAT)
    col_blocks = source_blocks.shape[0]

    def forward_step(total, values, rows_here, cols_here, live):
        inputs = jnp.take(source_blocks, cols_here, axis=0)
        product = jnp.einsum("tij,tjf->tif", values, inputs, preferred_element_type=jnp.float32)
        product = product * live.astype(jnp.float32)[:, None, None]
        return total.at[rows_here].add(product)

    dest_part = run_tiles(
        locate, own_count, forward_step, jnp.zeros((row_blocks, BLOCK, FEAT), jnp.float32)
    )
    agg = lax.psum_scatter(
        dest_part.reshape(row_blocks * BLOCK, FEAT), ("col", "rep"), scatter_dimension=0, tiled=True
    )
    agg_b = agg.astype(jnp.bfloat16)
    keep = relu_mask.astype(jnp.float32)
    hidden = jnp.dot(agg_b, weight, preferred_element_type=jnp.float32)
    activated = (hidden * keep).astype(jnp.bfloat16)
    grad_h = (cotangent.astype(jnp.float32) * keep).astype(jnp.bfloat16)
    weight_term = lax.dot_general(
        agg_b, grad_h, (((0,), (0,)), ((), ())), preferred_element_type=jnp.float32
    )
    node_total = node_dev * row_count * lax.axis_size("col") * rep_count
    grad_w = lax.psum(weight_term, ("row", "col", "rep")) * float(node_total) ** (-0.5)
    back = lax.dot_general(
        grad_h, weight, (((1,), (1,)), ((), ())), preferred_element_type=jnp.float32
    ).astype(jnp.bfloat16)
    dest_blocks = lax.all_gather(back, ("col", "rep"), axis=0, tiled=True).reshape(
        row_blocks, BLOCK, FEAT
    )

    def backward_step(total, values, rows_here, cols_here, live):
        inputs = jnp.take(dest_blocks, rows_here, axis=0)
        product = jnp.einsum("tij,tif->tjf", values, inputs, preferred_element_type=jnp.float32)
        product = product * live.astype(jnp.float32)[:, None, None]
        return total.at[cols_here].add(product)

    source_part = run_tiles(
        locate, own_count, backward_step, jnp.zeros((col_blocks, BLOCK, FEAT), jnp.float32)
    )
    grad_acc = lax.psum_scatter(
        source_part.reshape(col_blocks * BLOCK, FEAT),
        ("row", "rep"),
        scatter_dimension=0,
        tiled=True,
    )
    return (activated, grad_w, grad_acc.astype(jnp.bfloat16))


def solution(mesh):
    sizes = tuple(mesh.shape[name] for name in ("row", "col", "rep"))
    spread = ("parts", "row", "col", "rep")
    placed = (
        P(spread, None), P(), P(spread, None, None), P(spread), P(spread), P(spread),
        P(spread, None), P(spread, None),
    )

    def whole(*args):
        local = functools.partial(fused_body, *sizes) if fits(mesh, args) else body
        return jax.shard_map(
            local,
            mesh=mesh,
            in_specs=placed,
            out_specs=(P(spread, None), P("parts", None), P(spread, None)),
            check_vma=False,
        )(*args)

    return whole
```

```python
import functools

import jax
import jax.numpy as jnp
from jax import lax
from jax.experimental import pallas as pl
from jax.experimental.pallas import tpu as pltpu
from jax.sharding import PartitionSpec as P

FEAT = 128
BLOCK = 128
LANES = 128
SUBROWS = 16
VMEM_LIMIT = 60 * 1024 * 1024


def fused(
    rows_n, cols_n, reps_n, scale,
    feats, weight, tiles, tile_rows, tile_cols, count, mask, cot,
    act_o, gw_o, gx_o,
    wv, tv, mv, cv, rv, kv, idx_v, idx_s, chain, a_send, a_recv, a_mat,
    f_buf, b_buf, agg_s, agg_r, gx_s, gx_r, gw_s, gw_r, gw_z, gw_b, act_v, gx_v,
    loc, idx_sem, fs, fr, bs, br, as_, ar, gs, gr, xs, xr, ws1, wr1, ws2, wr2, ws3, wr3,
):
    part = lax.axis_index("parts")
    r = lax.axis_index("row")
    c = lax.axis_index("col")
    p = lax.axis_index("rep")
    plane = cols_n * reps_n
    q = c * reps_n + p
    slots = tiles.shape[0]
    row_blocks = plane
    col_blocks = rows_n * reps_n

    def remote(src, dst, send, recv, device):
        return pltpu.make_async_remote_copy(
            src_ref=src, dst_ref=dst, send_sem=send, recv_sem=recv,
            device_id=device, device_id_type=pl.DeviceIdType.MESH,
        )

    barrier = pltpu.get_barrier_semaphore()

    def plane_peer(k):
        other = lax.rem(q + k, plane)
        return other, (part, r, other // reps_n, other % reps_n)

    def row_peer(k):
        other = lax.rem(r + k, rows_n)
        return other, (part, other, c, p)

    for k in range(1, plane):
        pl.semaphore_signal(
            barrier, inc=1, device_id=plane_peer(k)[1], device_id_type=pl.DeviceIdType.MESH
        )
    for k in range(1, rows_n):
        pl.semaphore_signal(
            barrier, inc=1, device_id=row_peer(k)[1], device_id_type=pl.DeviceIdType.MESH
        )

    own_feats = f_buf.at[pl.ds(pl.multiple_of(r * BLOCK, BLOCK), BLOCK)]
    loads = [
        pltpu.make_async_copy(src, dst, loc.at[i])
        for i, (src, dst) in enumerate(
            [(tile_rows, rv), (tile_cols, kv), (mask, mv), (cot, cv), (weight, wv),
             (feats, own_feats), (tiles, tv)]
        )
    ]
    for copy in loads[5:6] + loads[:5] + loads[6:]:
        copy.start()

    loads[5].wait()
    pl.semaphore_wait(barrier, plane + rows_n - 2)

    f_copies = []
    for k in range(1, rows_n):
        copy = remote(
            own_feats, own_feats, fs.at[k], fr.at[k],
            (part, lax.rem(r + k, rows_n), c, p),
        )
        copy.start()
        f_copies.append(copy)

    loads[0].wait()
    loads[1].wait()
    key = rv[...] * col_blocks + kv[...]
    shape = (slots, LANES)
    lane = lax.broadcasted_iota(jnp.int32, shape, 1)
    sub = lax.broadcasted_iota(jnp.int32, shape, 0)
    wide = jnp.concatenate([key, jnp.full((1, LANES - slots), -1, jnp.int32)], axis=1)
    wide = jnp.broadcast_to(wide, shape)
    tall = jnp.sum(jnp.where(lane == sub, wide, 0), axis=1, keepdims=True)
    prev = jnp.where((tall == wide) & (sub < lane), sub + 1, 0)
    last = jnp.where((tall == lane) & (sub < count[0]), sub + 1, 0)
    idx_v[...] = jnp.zeros_like(idx_v)
    idx_v[0:1, :] = jnp.max(prev, axis=0, keepdims=True)
    idx_v[1:2, :] = jnp.max(last, axis=0, keepdims=True)
    idx_copy = pltpu.make_async_copy(idx_v, idx_s, idx_sem)
    idx_copy.start()

    for copy in loads[2:5]:
        copy.wait()
    keep = mv[...].astype(jnp.float32)
    grad_h = (cv[...].astype(jnp.float32) * keep).astype(jnp.bfloat16)
    b_buf[q] = lax.dot_general(
        wv[...], grad_h, (((1,), (1,)), ((), ())), preferred_element_type=jnp.float32
    ).astype(jnp.bfloat16)

    b_copies = []
    for k in range(1, plane):
        other = lax.rem(q + k, plane)
        copy = remote(
            b_buf.at[q], b_buf.at[q], bs.at[k], br.at[k],
            (part, r, other // reps_n, other % reps_n),
        )
        copy.start()
        b_copies.append(copy)

    loads[6].wait()
    idx_copy.wait()
    chain[0] = jnp.zeros((BLOCK, BLOCK), jnp.float32)

    @pl.loop(0, slots)
    def _(t):
        chain[t + 1] = chain[idx_s[0, t]] + tv[t].astype(jnp.float32)

    chunk = reps_n * BLOCK
    a_copies = []
    for k in range(cols_n):
        dest = lax.rem(c + 1 + k, cols_n)
        for j in range(reps_n):
            for i in range(rows_n):
                cell = (dest * reps_n + j) * col_blocks + i * reps_n + (1 - p)
                a_send[k, pl.ds(j * BLOCK, BLOCK), pl.ds(i * BLOCK, BLOCK)] = chain[
                    idx_s[1, cell]
                ].astype(jnp.bfloat16)
        copy = remote(a_send.at[k], a_recv.at[k], as_.at[k], ar.at[k], (part, r, c, 1 - p))
        copy.start()
        a_copies.append(copy)

    for k in range(cols_n):
        dest = lax.rem(c + 1 + k, cols_n)
        a_copies[k].wait_recv()
        for j in range(reps_n):
            for i in range(rows_n):
                cell = (dest * reps_n + j) * col_blocks + i * reps_n + p
                spot = (pl.ds(j * BLOCK, BLOCK), pl.ds(i * BLOCK, BLOCK))
                a_mat[(k, *spot)] = (
                    chain[idx_s[1, cell]] + a_recv[(k, *spot)].astype(jnp.float32)
                ).astype(jnp.bfloat16)

    for copy in f_copies:
        copy.wait_recv()
    g_copies = []
    for k in range(cols_n):
        dest = lax.rem(c + 1 + k, cols_n)
        partial = jnp.dot(
            a_mat[k], f_buf[...], preferred_element_type=jnp.float32
        ).astype(jnp.bfloat16)
        for j in range(reps_n):
            agg_s[k * reps_n + j] = partial[j * BLOCK:(j + 1) * BLOCK]
        targets = range(reps_n) if k < cols_n - 1 else [1 - p]
        for j in targets:
            copy = remote(
                agg_s.at[k * reps_n + j], agg_r.at[q], gs.at[k * reps_n + j], gr.at[q],
                (part, r, dest, j),
            )
            copy.start()
            g_copies.append(copy)

    for copy in b_copies:
        copy.wait_recv()
    grad_t = jnp.zeros((FEAT, rows_n * BLOCK), jnp.float32)
    for k in range(cols_n):
        dest = lax.rem(c + 1 + k, cols_n)
        pair = jnp.concatenate([b_buf[dest * reps_n + j] for j in range(reps_n)], axis=1)
        grad_t += jnp.dot(pair, a_mat[k], preferred_element_type=jnp.float32)
    for i in range(rows_n):
        gx_s[i] = grad_t[:, i * BLOCK:(i + 1) * BLOCK].astype(jnp.bfloat16)
    x_copies = []
    for k in range(1, rows_n):
        other = lax.rem(r + k, rows_n)
        copy = remote(gx_s.at[other], gx_r.at[k], xs.at[k], xr.at[k], (part, other, c, p))
        copy.start()
        x_copies.append(copy)

    agg = agg_s[(cols_n - 1) * reps_n + p].astype(jnp.float32)
    for k in range(1, plane):
        other = lax.rem(q + k, plane)
        remote(agg_s.at[0], agg_r.at[other], gs.at[0], gr.at[other], (part, r, c, 1 - p)).wait_recv()
        agg += agg_r[other].astype(jnp.float32)
    agg_b = agg.astype(jnp.bfloat16)
    term = lax.dot_general(
        agg_b, grad_h, (((0,), (0,)), ((), ())), preferred_element_type=jnp.float32
    ).astype(jnp.bfloat16)
    piece = FEAT // plane
    for i in range(plane):
        gw_s[i] = term[i * piece:(i + 1) * piece]
    w_copies = []
    for k in range(1, plane):
        other, device = plane_peer(k)
        copy = remote(gw_s.at[other], gw_r.at[k], ws1.at[k], wr1.at[k], device)
        copy.start()
        w_copies.append(copy)

    hidden = jnp.dot(agg_b, wv[...], preferred_element_type=jnp.float32)
    act_v[...] = (hidden * keep).astype(jnp.bfloat16)
    stores = [
        pltpu.make_async_copy(act_v, act_o, loc.at[0]),
        pltpu.make_async_copy(gx_v, gx_o, loc.at[1]),
    ]
    stores[0].start()

    slab = gw_s[q].astype(jnp.float32)
    for k in range(1, plane):
        w_copies[k - 1].wait_recv()
        slab += gw_r[k].astype(jnp.float32)
    gw_z[r] = slab
    z_copies = []
    for k in range(1, rows_n):
        copy = remote(gw_z.at[r], gw_z.at[r], ws2.at[k], wr2.at[k], row_peer(k)[1])
        copy.start()
        z_copies.append(copy)
    for copy in z_copies:
        copy.wait_recv()
    gw_b[q] = (jnp.sum(gw_z[...], axis=0) * scale).astype(jnp.bfloat16)
    o_copies = []
    for k in range(1, plane):
        copy = remote(gw_b.at[q], gw_b.at[q], ws3.at[k], wr3.at[k], plane_peer(k)[1])
        copy.start()
        o_copies.append(copy)

    grad_t = gx_s[r].astype(jnp.float32)
    for k, copy in enumerate(x_copies):
        copy.wait_recv()
        grad_t += gx_r[k + 1].astype(jnp.float32)
    gx_v[...] = grad_t.T.astype(jnp.bfloat16)
    stores[1].start()

    for copy in o_copies:
        copy.wait_recv()
    stores.append(pltpu.make_async_copy(gw_b, gw_o, loc.at[2]))
    stores[2].start()

    for copy in w_copies + z_copies + o_copies:
        copy.wait_send()
    for copy in stores:
        copy.wait()
    for copy in f_copies + b_copies + a_copies + g_copies + x_copies:
        copy.wait_send()


def hand_over(act, gw, gx, act_o, gw_o, gx_o, act_v, gw_v, gx_v, wide_v, sems):
    loads = [
        pltpu.make_async_copy(src, dst, sems.at[i])
        for i, (src, dst) in enumerate([(gw, gw_v), (act, act_v), (gx, gx_v)])
    ]
    stores = [
        pltpu.make_async_copy(src, dst, sems.at[3 + i])
        for i, (src, dst) in enumerate([(wide_v, gw_o), (act_v, act_o), (gx_v, gx_o)])
    ]
    for copy in loads:
        copy.start()
    loads[0].wait()
    piece = gw_v.shape[1]
    for i in range(gw_v.shape[0]):
        wide_v[i * piece:(i + 1) * piece, :] = gw_v[i].astype(jnp.float32)
    stores[0].start()
    for load, store in zip(loads[1:], stores[1:]):
        load.wait()
        store.start()
    for copy in stores:
        copy.wait()


def fused_body(rows_n, cols_n, reps_n, *args):
    feats, weight, tiles, tile_rows, tile_cols, count, mask, cot = args
    slots = tiles.shape[0]
    hid = weight.shape[1]
    plane = cols_n * reps_n
    total = rows_n * plane
    nodes = feats.shape[0] * total
    half = rows_n * BLOCK
    b16, f32, i32 = jnp.bfloat16, jnp.float32, jnp.int32
    dma = pltpu.SemaphoreType.DMA
    anywhere = pl.BlockSpec(memory_space=pl.ANY)
    results = pl.pallas_call(
        functools.partial(fused, rows_n, cols_n, reps_n, float(nodes) ** -0.5),
        out_shape=(
            jax.ShapeDtypeStruct((BLOCK, hid), b16),
            jax.ShapeDtypeStruct((plane, FEAT // plane, hid), b16),
            jax.ShapeDtypeStruct((BLOCK, FEAT), b16),
        ),
        in_specs=[anywhere] * 5 + [pl.BlockSpec(memory_space=pltpu.SMEM)] + [anywhere] * 2,
        out_specs=(anywhere,) * 3,
        scratch_shapes=[
            pltpu.VMEM((FEAT, hid), b16),
            pltpu.VMEM((slots, BLOCK, BLOCK), b16),
            pltpu.VMEM((BLOCK, hid), i32),
            pltpu.VMEM((BLOCK, hid), b16),
            pltpu.VMEM((1, slots), i32),
            pltpu.VMEM((1, slots), i32),
            pltpu.VMEM((8, LANES), i32),
            pltpu.SMEM((8, LANES), i32),
            pltpu.VMEM((slots + 1, BLOCK, BLOCK), f32),
            pltpu.VMEM((cols_n, reps_n * BLOCK, half), b16),
            pltpu.VMEM((cols_n, reps_n * BLOCK, half), b16),
            pltpu.VMEM((cols_n, reps_n * BLOCK, half), b16),
            pltpu.VMEM((half, FEAT), b16),
            pltpu.VMEM((plane, FEAT, BLOCK), b16),
            pltpu.VMEM((plane, BLOCK, FEAT), b16),
            pltpu.VMEM((plane, BLOCK, FEAT), b16),
            pltpu.VMEM((rows_n, FEAT, BLOCK), b16),
            pltpu.VMEM((rows_n, FEAT, BLOCK), b16),
            pltpu.VMEM((plane, FEAT // plane, hid), b16),
            pltpu.VMEM((plane, FEAT // plane, hid), b16),
            pltpu.VMEM((rows_n, FEAT // plane, hid), f32),
            pltpu.VMEM((plane, FEAT // plane, hid), b16),
            pltpu.VMEM((BLOCK, hid), b16),
            pltpu.VMEM((BLOCK, FEAT), b16),
            dma((7,)), dma,
            dma((rows_n,)), dma((rows_n,)),
            dma((plane,)), dma((plane,)),
            dma((cols_n,)), dma((cols_n,)),
            dma((plane,)), dma((plane,)),
            dma((rows_n,)), dma((rows_n,)),
            dma((plane,)), dma((plane,)),
            dma((rows_n,)), dma((rows_n,)),
            dma((plane,)), dma((plane,)),
        ],
        compiler_params=pltpu.CompilerParams(
            collective_id=0, has_side_effects=True, vmem_limit_bytes=VMEM_LIMIT
        ),
    )(
        feats, weight, tiles, tile_rows.reshape(1, slots), tile_cols.reshape(1, slots),
        count, mask, cot,
    )
    return tuple(pl.pallas_call(
        hand_over,
        out_shape=(
            jax.ShapeDtypeStruct((BLOCK, hid), b16),
            jax.ShapeDtypeStruct((FEAT, hid), f32),
            jax.ShapeDtypeStruct((BLOCK, FEAT), b16),
        ),
        in_specs=[anywhere] * 3,
        out_specs=(anywhere,) * 3,
        scratch_shapes=[
            pltpu.VMEM((BLOCK, hid), b16),
            pltpu.VMEM((plane, FEAT // plane, hid), b16),
            pltpu.VMEM((BLOCK, FEAT), b16),
            pltpu.VMEM((FEAT, hid), f32),
            dma((6,)),
        ],
        compiler_params=pltpu.CompilerParams(vmem_limit_bytes=VMEM_LIMIT),
    )(*results))


def fits(mesh, args):
    rows_n, cols_n, reps_n = (mesh.shape[name] for name in ("row", "col", "rep"))
    total = rows_n * cols_n * reps_n
    cells = rows_n * reps_n * cols_n * reps_n
    return (
        reps_n == 2
        and cells <= LANES
        and args[2].shape[0] // (total * mesh.shape["parts"]) <= LANES // 2
        and args[0].shape[0] == total * BLOCK * mesh.shape["parts"]
        and FEAT % (SUBROWS * cols_n * reps_n) == 0
    )


tiles_per_turn = 4


def run_tiles(locate, finish, step_fn, init):
    turns = (finish + tiles_per_turn - 1) // tiles_per_turn

    def turn(index, carry):
        slots = index * tiles_per_turn + jnp.arange(tiles_per_turn, dtype=jnp.int32)
        live = slots < finish
        values, rows_here, cols_here = locate(slots)
        return step_fn(carry, values, rows_here, cols_here, live)

    return lax.fori_loop(0, turns, turn, init)


def body(feats, weight, tile_vals, tile_rows, tile_cols, tile_count, relu_mask, cotangent):
    slot_total = tile_vals.shape[0]
    rep_count = lax.axis_size("rep")
    row_count = lax.axis_size("row")
    node_dev = feats.shape[0]
    row_blocks = node_dev * lax.axis_size("col") * rep_count // BLOCK
    own_count = tile_count[0]

    def locate(slots):
        place = jnp.minimum(slots, slot_total - 1)
        return (
            jnp.take(tile_vals, place, axis=0),
            jnp.take(tile_rows, place),
            jnp.take(tile_cols, place),
        )

    gathered = lax.all_gather(feats, ("row", "rep"), axis=0, tiled=True)
    source_blocks = gathered.reshape(-1, BLOCK, FEAT)
    col_blocks = source_blocks.shape[0]

    def forward_step(total, values, rows_here, cols_here, live):
        inputs = jnp.take(source_blocks, cols_here, axis=0)
        product = jnp.einsum("tij,tjf->tif", values, inputs, preferred_element_type=jnp.float32)
        product = product * live.astype(jnp.float32)[:, None, None]
        return total.at[rows_here].add(product)

    dest_part = run_tiles(
        locate, own_count, forward_step, jnp.zeros((row_blocks, BLOCK, FEAT), jnp.float32)
    )
    agg = lax.psum_scatter(
        dest_part.reshape(row_blocks * BLOCK, FEAT), ("col", "rep"), scatter_dimension=0, tiled=True
    )
    agg_b = agg.astype(jnp.bfloat16)
    keep = relu_mask.astype(jnp.float32)
    hidden = jnp.dot(agg_b, weight, preferred_element_type=jnp.float32)
    activated = (hidden * keep).astype(jnp.bfloat16)
    grad_h = (cotangent.astype(jnp.float32) * keep).astype(jnp.bfloat16)
    weight_term = lax.dot_general(
        agg_b, grad_h, (((0,), (0,)), ((), ())), preferred_element_type=jnp.float32
    )
    node_total = node_dev * row_count * lax.axis_size("col") * rep_count
    grad_w = lax.psum(weight_term, ("row", "col", "rep")) * float(node_total) ** (-0.5)
    back = lax.dot_general(
        grad_h, weight, (((1,), (1,)), ((), ())), preferred_element_type=jnp.float32
    ).astype(jnp.bfloat16)
    dest_blocks = lax.all_gather(back, ("col", "rep"), axis=0, tiled=True).reshape(
        row_blocks, BLOCK, FEAT
    )

    def backward_step(total, values, rows_here, cols_here, live):
        inputs = jnp.take(dest_blocks, rows_here, axis=0)
        product = jnp.einsum("tij,tif->tjf", values, inputs, preferred_element_type=jnp.float32)
        product = product * live.astype(jnp.float32)[:, None, None]
        return total.at[cols_here].add(product)

    source_part = run_tiles(
        locate, own_count, backward_step, jnp.zeros((col_blocks, BLOCK, FEAT), jnp.float32)
    )
    grad_acc = lax.psum_scatter(
        source_part.reshape(col_blocks * BLOCK, FEAT),
        ("row", "rep"),
        scatter_dimension=0,
        tiled=True,
    )
    return (activated, grad_w, grad_acc.astype(jnp.bfloat16))


def solution(mesh):
    sizes = tuple(mesh.shape[name] for name in ("row", "col", "rep"))
    spread = ("parts", "row", "col", "rep")
    placed = (
        P(spread, None), P(), P(spread, None, None), P(spread), P(spread), P(spread),
        P(spread, None), P(spread, None),
    )

    def whole(*args):
        local = functools.partial(fused_body, *sizes) if fits(mesh, args) else body
        return jax.shard_map(
            local,
            mesh=mesh,
            in_specs=placed,
            out_specs=(P(spread, None), P("parts", None), P(spread, None)),
            check_vma=False,
        )(*args)

    return whole
```
